1024 devices in a mesh: dp: 64 (over z, x_hi, core), mp: 16 (over x_lo, y).
Axes of the slice: x: 8 (x_hi: 4, x_lo: 2; x = x_hi * 2 + x_lo), y: 8, z: 8, core: 2. Of those that a mesh axis runs over, the one named last changes fastest.
Arguments:
- normed: bfloat16 [16384, 3072], P(('dp', 'mp')), may hold values from -24 to 24
- w_query: bfloat16 [3072, 6144], P(None, 'mp'), may hold values from -0.109375 to 0.109375
- query_gain: float32 [6144], P('mp'), may hold values from 0.1 to 1.9
- query_cot: bfloat16 [16384, 6144], P('dp', 'mp'), may hold values from -1.5 to 1.5
Outputs:
- queries: bfloat16 [16384, 6144], P('dp', 'mp')
- normed_grad: bfloat16 [16384, 3072], P(('dp', 'mp'))
- weight_grad: float32 [3072, 6144], P('dp', 'mp')
The draws below stay inside these ranges and needn't reach their ends.
All inputs are finite; a program needn't handle non-finite values.
Results may differ from the reference program's by a relative error of at most 0.018.
Values may be sent and summed in bfloat16 or wider, within the bound.
A program may use at most 32 MiB of HBM per device.

```python
import jax
import jax.numpy as jnp
from jax import lax

D = 3072
HEAD = 128
TOK = 256
HD = 6144
TOKENS = 16384
N_DP = 64
N_MP = 16


def strengthened(entries, rng, source, target, parts, factor):
    owner, partner = [(jnp.arange(entries.shape[position]) // (entries.shape[position] // parts)).reshape([-1 if axis == position else 1 for axis in range(entries.ndim)]) for position in (source, target)]
    chosen = jax.random.permutation(rng, parts)[partner]
    strong = (owner == chosen) | (owner == (partner + parts // 2) % parts)
    return jnp.where(strong, factor * entries, entries)


def steps_of(key, shape, pieces, smallest, top_value):
    level, own = 1.0, jax.random.fold_in(key, 6)
    for dim, blocks in pieces:
        draws = jnp.exp(jax.random.uniform(jax.random.fold_in(own, dim), (blocks,), jnp.float32, smallest / len(pieces), top_value / len(pieces)))
        level = level * jnp.repeat(draws, shape[dim] // blocks).reshape([-1 if axis == dim else 1 for axis in range(len(shape))])
    return level


def noise(stream_key, dims, spread, most, cuts=(), held_as=jnp.bfloat16):
    array = spread * jax.random.normal(stream_key, dims, jnp.float32)
    if cuts:
        array = array * steps_of(stream_key, dims, cuts, -0.22, 0.18)
    return jnp.clip(array, -most, most).astype(held_as)


def gaussian_with(own_key, extent, spread, limit, cuts, heavy, held_as=jnp.bfloat16):
    result = spread * jax.random.normal(own_key, extent, jnp.float32)
    if cuts:
        result = result * steps_of(own_key, extent, cuts, -0.22, 0.18)
    return jnp.clip(strengthened(result, jax.random.fold_in(own_key, 3), *heavy), -limit, limit).astype(held_as)


def setup_inputs(seed: int = 0) -> dict:
    streams_of = jax.random.split(jax.random.key(seed), 5)
    normed = gaussian_with(streams_of[0], (TOKENS, D), 1.0, 24.0, ((0, 1024),), (0, 1, 1024, 6.0))
    w_query = noise(streams_of[1], (D, HD), D ** -0.5, 0.109375, ((1, 16),))
    query_gain = jnp.clip(1.0 + 0.18 * jax.random.normal(streams_of[2], (HD,), jnp.float32), 0.1, 1.9)
    query_cot = noise(streams_of[3], (TOKENS, HD), 0.25, 1.5, ((0, 64), (1, 16)))
    return {"normed": normed, "w_query": w_query, "query_gain": query_gain, "query_cot": query_cot}


def image_group(tokens_in, cot_in, w_query, query_gain):
    projected = jnp.dot(tokens_in, w_query, preferred_element_type=jnp.float32)
    tok_count = tokens_in.shape[0]
    heads_view = projected.reshape(tok_count, -1, HEAD)
    average = lax.optimization_barrier(jnp.mean(heads_view, axis=-1, keepdims=True))
    centred = heads_view - average
    spread_inv = lax.rsqrt(lax.optimization_barrier(jnp.mean(centred * centred, axis=-1, keepdims=True)) + 1e-06)
    unit = centred * spread_inv
    gain_view = query_gain.reshape(-1, HEAD)
    queries = (unit * gain_view).reshape(tok_count, -1).astype(jnp.bfloat16)
    scaled = cot_in.astype(jnp.float32).reshape(tok_count, -1, HEAD) * gain_view
    pre_grad = spread_inv * (scaled - lax.optimization_barrier(jnp.mean(scaled, axis=-1, keepdims=True)) - unit * lax.optimization_barrier(jnp.mean(scaled * unit, axis=-1, keepdims=True)))
    pre_grad = pre_grad.reshape(tok_count, -1).astype(jnp.bfloat16)
    grad_blocks = pre_grad.astype(jnp.float32).reshape(tok_count, N_MP, -1)
    weight_blocks = w_query.astype(jnp.float32).reshape(D, N_MP, -1)
    part_grad = jnp.einsum('tnc,dnc->ntd', grad_blocks, weight_blocks).astype(jnp.bfloat16)
    part_grad = lax.optimization_barrier(part_grad)
    normed_grad = lax.optimization_barrier(jnp.sum(part_grad.astype(jnp.float32), axis=0)).astype(jnp.bfloat16)
    group_grad = lax.dot_general(tokens_in, pre_grad, (((0,), (0,)), ((), ())), preferred_element_type=jnp.float32)
    return (queries, normed_grad, group_grad)

def reference(normed, w_query, query_gain, query_cot):
    token_groups = normed.reshape(N_DP, TOK, D)
    cot_groups = query_cot.reshape(N_DP, TOK, HD)

    def step_group(total, pair):
        queries, normed_grad, group_grad = image_group(pair[0], pair[1], w_query, query_gain)
        return (total + group_grad, (queries, normed_grad))
    weight_grad, outs = lax.scan(step_group, jnp.zeros((D, HD), jnp.float32), (token_groups, cot_groups))
    queries, normed_grad = outs
    return (queries.reshape(TOKENS, HD), normed_grad.reshape(TOKENS, D), weight_grad)
```

```python
import functools
import itertools

import jax
import jax.numpy as jnp
from jax import lax
from jax.experimental import pallas as pl
from jax.experimental.pallas import tpu as pltpu
from jax.sharding import PartitionSpec as P

HEAD = 128
PAIR = 2
CORES = 2
ACROSS = 4
MESH = pl.DeviceIdType.MESH
GATHER_XY = 2
GATHER_DIRECT = False
SCATTER_YX = 3


def sums(half):
    if half == 4:
        return [[(4, 2), (3, 2)], [(2, 1)], [(1, 0)]]
    return [[(k, k - 1)] for k in range(half, 0, -1)]


def blocks_by_turn(half):
    rounds = [[k * d for k, _ in edges for d in ((1,) if k == half else (1, -1))] for edges in sums(half)]
    return rounds + [[0]]


def spread(half):
    if half == 4 and GATHER_DIRECT:
        rounds = [[(0, 1), (0, 2)], [(2, 3), (2, 4)]]
    else:
        rounds = [[(b, a) for a, b in edges] for edges in reversed(sums(half))]
    children = {k: [b for edges in rounds for a, b in edges if a == k] for k in range(half + 1)}
    return children, [[b for _, b in edges] for edges in rounds]


def kernel(
    dims, normed, w_hbm, gain, cot_hbm, queries_out, grad_out, weight_out,
    tokens, turned, w, cot, proj, pre, terms, term_mine, term_sent, core_got,
    z_send, z_got, x_send, x_got, y_send, y_got, pair_got, last_send, last_got,
    local_sem, send_sem, recv_sem,
):
    ring_y, ring_z, rows, features, columns = dims
    half_y, half_z = ring_y // 2, ring_z // 2
    chunks, width = ring_z, features // ring_z
    own_rows = width // (ACROSS * CORES)
    tok = PAIR * ring_y * rows
    f32, bf16 = jnp.float32, jnp.bfloat16
    dp, mp = lax.axis_index("dp"), lax.axis_index("mp")
    pair, y = mp // ring_y, lax.rem(mp, ring_y)
    core = lax.rem(dp, CORES)
    across = lax.rem(dp // CORES, ACROSS)
    z = dp // (CORES * ACROSS)
    other_pair, other_core = 1 - pair, 1 - core

    def at_y(step):
        return lax.rem(y + step + ring_y, ring_y)

    def at_z(step):
        return lax.rem(z + step + ring_z, ring_z)

    def at_across(step):
        return lax.rem(across + step, ACROSS)

    def dp_of(zz, xx, cc):
        return (zz * ACROSS + xx) * CORES + cc

    to_pair = (dp, other_pair * ring_y + y)
    to_core = (dp_of(z, across, other_core), mp)
    steps_y, steps_z = [[-2, -1, 1, 2] if half > 2 else [-1, 1] for half in (half_y, half_z)]
    to_y = {k: (dp, pair * ring_y + at_y(k)) for k in steps_y}
    to_z = {k: (dp_of(at_z(k), across, core), mp) for k in steps_z}
    to_across = {j: (dp_of(z, at_across(j), core), mp) for j in range(1, ACROSS)}

    count = itertools.count()

    def remote(src, dst, device, group, i):
        return pltpu.make_async_remote_copy(
            src_ref=src, dst_ref=dst, send_sem=send_sem.at[group], recv_sem=recv_sem.at[i],
            device_id=device, device_id_type=MESH,
        )

    def send(src, dst, device, group, i=None):
        copy = remote(src, dst, device, group, next(count) if i is None else i)
        copy.start()
        return copy

    def wait_shared(view, i):
        remote(view, view, to_core, 0, i).wait_recv()

    def wait_group(group, view):
        remote(view, view, to_core, group, 0).wait_send()

    def length(half, index, d):
        return half if (d == 1) == (index % 2 == 0) else half - 1

    w_in = pltpu.make_async_copy(w_hbm, w, local_sem.at[1])
    cot_in = pltpu.make_async_copy(cot_hbm, cot, local_sem.at[2])
    for c in range(chunks):
        pltpu.make_async_copy(
            normed.at[:, pl.ds(c * width, width)], tokens.at[c, pair, y], local_sem.at[0]
        ).start()
    w_in.start()
    cot_in.start()

    barrier = pltpu.get_barrier_semaphore()
    peers = [to_pair, to_core, *to_y.values(), *to_z.values(), *to_across.values()]
    for peer in peers:
        pl.semaphore_signal(barrier, inc=1, device_id=peer, device_id_type=MESH)
    own = tokens.at[:, pair, y]
    pltpu.make_async_copy(own, own, local_sem.at[0]).wait()
    pl.semaphore_wait(barrier, len(peers))

    children, arrivals = spread(half_y)

    def onward(views, k, d, c, group):
        return {
            t: [send(view, view, to_y[d * (t - k)], group) for view in views]
            for t in children[k]
            if t <= length(half_y, c, d)
        }

    def gather_xy(c):
        mine, theirs = tokens.at[c, pair, y], tokens.at[c, other_pair, y]
        over = send(mine, mine, to_pair, 0)
        chain = {d: onward([mine], 0, d, c, 1) for d in (1, -1)}
        yield
        over.wait_recv()
        for d in chain:
            for t, copies in onward([theirs], 0, d, c, 1).items():
                chain[d][t] += copies
        yield
        for now in arrivals:
            for t in now:
                for d in chain:
                    if t in chain[d]:
                        for copy in chain[d][t]:
                            copy.wait_recv()
                        chain[d].update(onward([tokens.at[c, :, at_y(-d * t)]], t, d, c, 1))
            yield

    def gather_yx(c):
        mine = tokens.at[c, pair, y]
        chain = {d: onward([mine], 0, d, c, 2) for d in (1, -1)}
        over = [send(mine, mine, to_pair, 3)]
        yield
        for now in arrivals:
            for t in now:
                for d in chain:
                    if t in chain[d]:
                        chain[d][t][0].wait_recv()
                        view = tokens.at[c, pair, at_y(-d * t)]
                        chain[d].update(onward([view], t, d, c, 2))
                        over.append(send(view, view, to_pair, 3))
            yield
        for copy in over:
            copy.wait_recv()

    def project(c):
        got = tokens[c].reshape(tok, width)
        term = jnp.dot(got, w[pl.ds(c * width, width), :], preferred_element_type=f32)
        if c == 0:
            proj[...] = term
        else:
            proj[...] += term
        turned[c] = got.T

    gathers = [(gather_xy if c < GATHER_XY else gather_yx)(c) for c in range(chunks)]
    for _ in range(len(arrivals) + 2):
        for g in gathers[GATHER_XY:] + gathers[:GATHER_XY]:
            next(g, None)
    w_in.wait()
    for c in range(chunks):
        for _ in gathers[c]:
            pass
        project(c)

    cot_in.wait()
    for head in range(columns // HEAD):
        cols = pl.ds(head * HEAD, HEAD)
        values = proj[:, cols]
        centred = values - jnp.mean(values, axis=-1, keepdims=True)
        spread_inv = lax.rsqrt(jnp.mean(centred * centred, axis=-1, keepdims=True) + 1e-06)
        unit = centred * spread_inv
        queries_out[:, cols] = (unit * gain[cols]).astype(bf16)
        scaled = cot[:, cols].astype(f32) * gain[cols]
        grad = spread_inv * (
            scaled
            - jnp.mean(scaled, axis=-1, keepdims=True)
            - unit * jnp.mean(scaled * unit, axis=-1, keepdims=True)
        )
        pre[:, cols] = grad.astype(bf16)

    core_copy = {}

    def slot(step):
        return step % ring_z

    def weight_term(step):
        i = slot(step)
        term = jnp.dot(turned[at_z(step)], pre[...], preferred_element_type=f32)
        term = term.reshape(ACROSS, CORES, own_rows, columns)
        term_mine[i] = term
        term_sent[i] = term.astype(bf16)
        core_copy[i] = send(term_sent.at[i, :, other_core], core_got.at[i], to_core, 8)

    arrived = set()

    def chip_term(step, block):
        i = slot(step)
        if i not in arrived:
            arrived.add(i)
            core_copy[i].wait_recv()
        return term_mine[i, block, core] + core_got[i, block].astype(f32)

    order_across = [2, 1, 3, 0][:ACROSS] if ACROSS == 4 else list(range(ACROSS - 1, -1, -1))

    def z_sum(chain, k, d, block):
        value = 0.0
        for n, copy in chain.get(k, []):
            copy.wait_recv()
            value = value + z_got[n, block].astype(f32)
        return value

    def weight_ring():
        chain = {(j, d): {} for j in order_across for d in (1, -1)}
        for edges in sums(half_z):
            for index, j in enumerate(order_across):
                block = at_across(j)
                for k, k_to in edges:
                    for d in (1, -1):
                        if k > length(half_z, index, d):
                            continue
                        n = k - 1 + (0 if d == 1 else half_z)
                        value = chip_term(d * k, block) + z_sum(chain[j, d], k, d, block)
                        z_send[n, block] = value.astype(bf16)
                        copy = send(z_send.at[n, block], z_got.at[n, block], to_z[d * (k - k_to)], 9)
                        chain[j, d].setdefault(k_to, []).append((n, copy))
            yield
        over = {}
        for index, j in enumerate(order_across):
            block = at_across(j)
            value = chip_term(0, block)
            for d in (1, -1):
                value = value + z_sum(chain[j, d], 0, d, block)
            if j:
                x_send[j - 1] = value.astype(bf16)
                over[j] = send(x_send.at[j - 1], x_got.at[j - 1], to_across[j], 10)
            else:
                total = value
        yield
        for j, copy in over.items():
            copy.wait_recv()
            total = total + x_got[j - 1].astype(f32)
        weight_out[...] = total

    def scatter(c):
        y_first = c < SCATTER_YX
        cols = pl.ds(c * width, width)
        term = lax.dot_general(
            pre[...], w[cols, :], (((1,), (1,)), ((), ())), preferred_element_type=f32
        )
        terms[c] = term.astype(bf16).reshape(PAIR, ring_y, rows, width)
        pieces = pl.ds(0, PAIR) if y_first else 0
        group = 4 if y_first else 6

        def local_term(step):
            if y_first:
                return terms[c, :, at_y(step)].astype(f32)
            return terms[c, pair, at_y(step)].astype(f32) + pair_got[c, at_y(step)].astype(f32)

        if not y_first:
            over = [(next(count), block) for block in blocks_by_turn(half_y)]
            for turn, (i, block) in enumerate(over):
                if turn == 1:
                    yield
                for r in block:
                    send(terms.at[c, other_pair, at_y(r)], pair_got.at[c, at_y(r)], to_pair, 7, i)
            yield
        chain = {d: {} for d in (1, -1)}

        def y_sum(k, d, piece):
            value = 0.0
            for n in chain[d].get(k, []):
                value = value + y_got[c, n, piece].astype(f32)
            return value

        def y_wait(k, d):
            for copy in copies.pop((k, d), []):
                copy.wait_recv()

        copies = {}
        for turn, edges in enumerate(sums(half_y)):
            if not y_first:
                i, block = over[turn]
                wait_shared(pair_got.at[c, pl.ds(0, len(block))], i)
            for k, k_to in edges:
                for d in (1, -1):
                    if k > length(half_y, c, d):
                        continue
                    n = k - 1 + (0 if d == 1 else half_y)
                    y_wait(k, d)
                    value = local_term(d * k) + y_sum(k, d, pieces)
                    y_send[c, n, pieces] = value.astype(bf16)
                    copy = send(
                        y_send.at[c, n, pieces], y_got.at[c, n, pieces], to_y[d * (k - k_to)], group
                    )
                    chain[d].setdefault(k_to, []).append(n)
                    copies.setdefault((k_to, d), []).append(copy)
            yield
        for d in (1, -1):
            y_wait(0, d)
        if y_first:
            def total(piece):
                return terms[c, piece, y].astype(f32) + y_sum(0, 1, piece) + y_sum(0, -1, piece)

            last_send[c] = total(other_pair).astype(bf16)
            over = send(last_send.at[c], last_got.at[c], to_pair, 5)
            yield
            over.wait_recv()
            value = total(pair) + last_got[c].astype(f32)
        else:
            i, block = over[-1]
            wait_shared(pair_got.at[c, pl.ds(0, len(block))], i)
            value = local_term(0) + y_sum(0, 1, 0) + y_sum(0, -1, 0)
        grad_out[:, cols] = value.astype(bf16)

    near = list(range(half_z - 2, 0, -1))
    weight_term(half_z)
    for d in (1, -1):
        if half_z > 1:
            weight_term(d * (half_z - 1))
    ring = weight_ring()
    next(ring)
    running = []
    for c in range(chunks):
        g = scatter(c)
        next(g)
        running.append(g)
        if near and c == chunks // 2:
            for d in (1, -1):
                weight_term(d * near[0])
    for g in running[SCATTER_YX:]:
        next(g)
    for k in near[1:]:
        for d in (1, -1):
            weight_term(d * k)
    weight_term(0)
    running.insert(0, ring)
    while running:
        for g in list(running):
            if next(g, running) is running:
                running.remove(g)

    far = ring_y - 1
    wait_group(0, tokens.at[pl.ds(0, GATHER_XY), 0, 0])
    wait_group(1, tokens.at[pl.ds(0, GATHER_XY), :, pl.ds(0, far)])
    wait_group(2, tokens.at[pl.ds(GATHER_XY, chunks - GATHER_XY), 0, pl.ds(0, far)])
    wait_group(3, tokens.at[pl.ds(GATHER_XY, chunks - GATHER_XY), 0])
    wait_group(4, terms.at[pl.ds(0, SCATTER_YX), :, pl.ds(0, far)])
    wait_group(5, terms.at[pl.ds(0, SCATTER_YX), 0, 0])
    wait_group(6, terms.at[pl.ds(SCATTER_YX, chunks - SCATTER_YX), 0, pl.ds(0, far)])
    wait_group(7, terms.at[pl.ds(SCATTER_YX, chunks - SCATTER_YX), 0])
    wait_group(8, core_got)
    wait_group(9, core_got.at[pl.ds(0, ring_z - 1)])
    wait_group(10, x_send)


def local(normed, w_query, query_gain, query_cot):
    ring_y = lax.axis_size("mp") // PAIR
    ring_z = lax.axis_size("dp") // (CORES * ACROSS)
    rows, features = normed.shape
    tok, columns = query_cot.shape
    chunks, width = ring_z, features // ring_z
    own_rows = width // (ACROSS * CORES)
    bf16, f32 = jnp.bfloat16, jnp.float32
    vmem, hbm = pl.BlockSpec(memory_space=pltpu.VMEM), pl.BlockSpec(memory_space=pltpu.HBM)
    y_count, z_count = ring_y - 1, ring_z - 1
    children, _ = spread(ring_y // 2)
    first = sum(t <= m for m in (ring_y // 2, ring_y // 2 - 1) for t in children[0])
    copies = GATHER_XY * (1 + y_count + first) + (chunks - GATHER_XY) * (2 * y_count + 1)
    copies += SCATTER_YX * (y_count + 1) + ring_z + ACROSS * z_count + ACROSS - 1
    copies += (chunks - SCATTER_YX) * (y_count + len(blocks_by_turn(ring_y // 2)))
    return pl.pallas_call(
        functools.partial(kernel, (ring_y, ring_z, rows, features, columns)),
        out_shape=(
            jax.ShapeDtypeStruct((tok, columns), bf16),
            jax.ShapeDtypeStruct((rows, features), bf16),
            jax.ShapeDtypeStruct((own_rows, columns), f32),
        ),
        in_specs=[hbm, hbm, vmem, hbm],
        out_specs=(vmem, vmem, vmem),
        scratch_shapes=[
            pltpu.VMEM((chunks, PAIR, ring_y, rows, width), bf16),
            pltpu.VMEM((chunks, width, tok), bf16),
            pltpu.VMEM((features, columns), bf16),
            pltpu.VMEM((tok, columns), bf16),
            pltpu.VMEM((tok, columns), f32),
            pltpu.VMEM((tok, columns), bf16),
            pltpu.VMEM((chunks, PAIR, ring_y, rows, width), bf16),
            pltpu.VMEM((ring_z, ACROSS, CORES, own_rows, columns), f32),
            pltpu.VMEM((ring_z, ACROSS, CORES, own_rows, columns), bf16),
            pltpu.VMEM((ring_z, ACROSS, own_rows, columns), bf16),
            pltpu.VMEM((ring_z, ACROSS, own_rows, columns), bf16),
            pltpu.VMEM((ring_z, ACROSS, own_rows, columns), bf16),
            pltpu.VMEM((ACROSS - 1, own_rows, columns), bf16),
            pltpu.VMEM((ACROSS - 1, own_rows, columns), bf16),
            pltpu.VMEM((chunks, ring_y, PAIR, rows, width), bf16),
            pltpu.VMEM((chunks, ring_y, PAIR, rows, width), bf16),
            pltpu.VMEM((chunks, ring_y, rows, width), bf16),
            pltpu.VMEM((chunks, rows, width), bf16),
            pltpu.VMEM((chunks, rows, width), bf16),
            pltpu.SemaphoreType.DMA((3,)),
            pltpu.SemaphoreType.DMA((11,)),
            pltpu.SemaphoreType.DMA((copies,)),
        ],
        compiler_params=pltpu.CompilerParams(
            collective_id=0, has_side_effects=True, vmem_limit_bytes=44 * 2**20
        ),
    )(*(pltpu.with_memory_space_constraint(a, pltpu.HBM) for a in (normed, w_query, query_gain, query_cot)))


def solution(mesh):
    return jax.shard_map(
        local,
        mesh=mesh,
        in_specs=(P(("dp", "mp"), None), P(None, "mp"), P("mp"), P("dp", "mp")),
        out_specs=(P("dp", "mp"), P(("dp", "mp"), None), P("dp", "mp")),
        check_vma=False,
    )
```

```python
import functools
import itertools

import jax
import jax.numpy as jnp
from jax import lax
from jax.experimental import pallas as pl
from jax.experimental.pallas import tpu as pltpu
from jax.sharding import PartitionSpec as P

HEAD = 128
PAIR = 2
CORES = 2
ACROSS = 4
MESH = pl.DeviceIdType.MESH
CHUNKS = 4
GATHER_XY = 1
SCATTER_YX = 2


def sums(half):
    if half == 4:
        return [[(4, 2), (3, 2)], [(2, 1)], [(1, 0)]]
    return [[(k, k - 1)] for k in range(half, 0, -1)]


def blocks_by_turn(half):
    rounds = [[k * d for k, _ in edges for d in ((1,) if k == half else (1, -1))] for edges in sums(half)]
    return rounds + [[0]]


def spread(half):
    rounds = [[(b, a) for a, b in edges] for edges in reversed(sums(half))]
    children = {k: [b for edges in rounds for a, b in edges if a == k] for k in range(half + 1)}
    return children, [[b for _, b in edges] for edges in rounds]


def kernel(
    dims, normed, w_hbm, gain, cot_hbm, queries_out, grad_out, weight_out,
    tokens, turned, w, cot, proj, pre, terms, term_mine, term_sent, core_got,
    z_send, z_got, x_send, x_got, y_send, y_got, pair_got, last_send, last_got,
    local_sem, send_sem, recv_sem,
):
    ring_y, ring_z, rows, features, columns = dims
    half_y, half_z = ring_y // 2, ring_z // 2
    chunks, width, group = CHUNKS, features // CHUNKS, features // ring_z
    own_rows = group // (ACROSS * CORES)
    tok = PAIR * ring_y * rows
    f32, bf16 = jnp.float32, jnp.bfloat16
    dp, mp = lax.axis_index("dp"), lax.axis_index("mp")
    pair, y = mp // ring_y, lax.rem(mp, ring_y)
    core = lax.rem(dp, CORES)
    across = lax.rem(dp // CORES, ACROSS)
    z = dp // (CORES * ACROSS)
    other_pair, other_core = 1 - pair, 1 - core

    def at_y(step):
        return lax.rem(y + step + ring_y, ring_y)

    def at_z(step):
        return lax.rem(z + step + ring_z, ring_z)

    def at_across(step):
        return lax.rem(across + step, ACROSS)

    def dp_of(zz, xx, cc):
        return (zz * ACROSS + xx) * CORES + cc

    to_pair = (dp, other_pair * ring_y + y)
    to_core = (dp_of(z, across, other_core), mp)
    steps_y, steps_z = [[-2, -1, 1, 2] if half > 2 else [-1, 1] for half in (half_y, half_z)]
    to_y = {k: (dp, pair * ring_y + at_y(k)) for k in steps_y}
    to_z = {k: (dp_of(at_z(k), across, core), mp) for k in steps_z}
    to_across = {j: (dp_of(z, at_across(j), core), mp) for j in range(1, ACROSS)}

    count = itertools.count()

    def remote(src, dst, device, group, i):
        return pltpu.make_async_remote_copy(
            src_ref=src, dst_ref=dst, send_sem=send_sem.at[group], recv_sem=recv_sem.at[i],
            device_id=device, device_id_type=MESH,
        )

    def send(src, dst, device, group, i=None):
        copy = remote(src, dst, device, group, next(count) if i is None else i)
        copy.start()
        return copy

    def wait_shared(view, i):
        remote(view, view, to_core, 0, i).wait_recv()

    def wait_group(group, view):
        remote(view, view, to_core, group, 0).wait_send()

    def length(half, index, d):
        return half if (d == 1) == (index % 2 == 0) else half - 1

    w_in = pltpu.make_async_copy(w_hbm, w, local_sem.at[1])
    cot_in = pltpu.make_async_copy(cot_hbm, cot, local_sem.at[2])
    for c in range(chunks):
        pltpu.make_async_copy(
            normed.at[:, pl.ds(c * width, width)], tokens.at[c, pair, y], local_sem.at[0]
        ).start()
    w_in.start()
    cot_in.start()

    barrier = pltpu.get_barrier_semaphore()
    peers = [to_pair, to_core, *to_y.values(), *to_z.values(), *to_across.values()]
    for peer in peers:
        pl.semaphore_signal(barrier, inc=1, device_id=peer, device_id_type=MESH)
    own = tokens.at[:, pair, y]
    pltpu.make_async_copy(own, own, local_sem.at[0]).wait()
    pl.semaphore_wait(barrier, len(peers))

    children, arrivals = spread(half_y)

    def onward(views, k, d, c, group):
        return {
            t: [send(view, view, to_y[d * (t - k)], group) for view in views]
            for t in children[k]
            if t <= length(half_y, c, d)
        }

    def gather_xy(c):
        mine, theirs = tokens.at[c, pair, y], tokens.at[c, other_pair, y]
        over = send(mine, mine, to_pair, 0)
        chain = {d: onward([mine], 0, d, c, 1) for d in (1, -1)}
        yield
        over.wait_recv()
        for d in chain:
            for t, copies in onward([theirs], 0, d, c, 1).items():
                chain[d][t] += copies
        yield
        for now in arrivals:
            for t in now:
                for d in chain:
                    if t in chain[d]:
                        for copy in chain[d][t]:
                            copy.wait_recv()
                        chain[d].update(onward([tokens.at[c, :, at_y(-d * t)]], t, d, c, 1))
            yield

    def gather_yx(c):
        mine = tokens.at[c, pair, y]
        chain = {d: onward([mine], 0, d, c, 2) for d in (1, -1)}
        over = next(count)
        send(mine, mine, to_pair, 3, over)
        yield
        for now in arrivals:
            for t in now:
                for d in chain:
                    if t in chain[d]:
                        chain[d][t][0].wait_recv()
                        view = tokens.at[c, pair, at_y(-d * t)]
                        chain[d].update(onward([view], t, d, c, 2))
                        send(view, view, to_pair, 3, over)
            yield
        wait_shared(tokens.at[c, other_pair], over)

    def project(c):
        got = tokens[c].reshape(tok, width)
        term = jnp.dot(got, w[pl.ds(c * width, width), :], preferred_element_type=f32)
        if c == 0:
            proj[...] = term
        else:
            proj[...] += term
        per = width // group
        turned[pl.ds(c * per, per)] = got.T.reshape(per, group, tok)

    gathers = [(gather_xy if c < GATHER_XY else gather_yx)(c) for c in range(chunks)]
    for _ in range(len(arrivals) + 2):
        for g in gathers[GATHER_XY:] + gathers[:GATHER_XY]:
            next(g, None)
    w_in.wait()
    for c in range(chunks):
        for _ in gathers[c]:
            pass
        project(c)

    cot_in.wait()
    for head in range(columns // HEAD):
        cols = pl.ds(head * HEAD, HEAD)
        values = proj[:, cols]
        centred = values - jnp.mean(values, axis=-1, keepdims=True)
        spread_inv = lax.rsqrt(jnp.mean(centred * centred, axis=-1, keepdims=True) + 1e-06)
        unit = centred * spread_inv
        queries_out[:, cols] = (unit * gain[cols]).astype(bf16)
        scaled = cot[:, cols].astype(f32) * gain[cols]
        grad = spread_inv * (
            scaled
            - jnp.mean(scaled, axis=-1, keepdims=True)
            - unit * jnp.mean(scaled * unit, axis=-1, keepdims=True)
        )
        pre[:, cols] = grad.astype(bf16)

    core_copy = {}

    def slot(step):
        return step % ring_z

    def weight_term(step):
        i = slot(step)
        term = jnp.dot(turned[at_z(step)], pre[...], preferred_element_type=f32)
        term = term.reshape(ACROSS, CORES, own_rows, columns)
        term_mine[i] = term
        term_sent[i] = term.astype(bf16)
        core_copy[i] = send(term_sent.at[i, :, other_core], core_got.at[i], to_core, 8)

    arrived = set()

    def chip_term(step, block):
        i = slot(step)
        if i not in arrived:
            arrived.add(i)
            core_copy[i].wait_recv()
        return term_mine[i, block, core] + core_got[i, block].astype(f32)

    order_across = [2, 1, 3, 0][:ACROSS] if ACROSS == 4 else list(range(ACROSS - 1, -1, -1))

    def z_sum(chain, k, d, block):
        value = 0.0
        for n, copy in chain.get(k, []):
            copy.wait_recv()
            value = value + z_got[n, block].astype(f32)
        return value

    def weight_ring():
        chain = {(j, d): {} for j in order_across for d in (1, -1)}
        rounds = sums(half_z)
        over = {}

        def one_round(index, turn):
            j = order_across[index]
            block = at_across(j)
            for k, k_to in (rounds + [[]])[turn]:
                for d in (1, -1):
                    if k > length(half_z, index, d):
                        continue
                    n = k - 1 + (0 if d == 1 else half_z)
                    value = chip_term(d * k, block) + z_sum(chain[j, d], k, d, block)
                    z_send[n, block] = value.astype(bf16)
                    copy = send(z_send.at[n, block], z_got.at[n, block], to_z[d * (k - k_to)], 9)
                    chain[j, d].setdefault(k_to, []).append((n, copy))
            if turn == len(rounds):
                value = chip_term(0, block)
                for d in (1, -1):
                    value = value + z_sum(chain[j, d], 0, d, block)
                if j:
                    x_send[j - 1] = value.astype(bf16)
                    over[j] = send(x_send.at[j - 1], x_got.at[j - 1], to_across[j], 10)
                else:
                    over[0] = value

        for turn in range(len(rounds) + 1):
            for index in range(ACROSS):
                one_round(index, turn)
            yield
        total = over.pop(0)
        for j, copy in over.items():
            copy.wait_recv()
            total = total + x_got[j - 1].astype(f32)
        weight_out[...] = total

    def scatter(c):
        y_first = c < SCATTER_YX
        cols = pl.ds(c * width, width)
        term = lax.dot_general(
            pre[...], w[cols, :], (((1,), (1,)), ((), ())), preferred_element_type=f32
        )
        terms[c] = term.astype(bf16).reshape(PAIR, ring_y, rows, width)
        pieces = pl.ds(0, PAIR) if y_first else 0
        sems = 4 if y_first else 6

        def local_term(step):
            if y_first:
                return terms[c, :, at_y(step)].astype(f32)
            return terms[c, pair, at_y(step)].astype(f32) + pair_got[c, at_y(step)].astype(f32)

        if not y_first:
            over = [(next(count), block) for block in blocks_by_turn(half_y)]
            for turn, (i, block) in enumerate(over):
                if turn == 1:
                    yield
                for r in block:
                    send(terms.at[c, other_pair, at_y(r)], pair_got.at[c, at_y(r)], to_pair, 7, i)
            yield
        chain = {d: {} for d in (1, -1)}

        def y_sum(k, d, piece):
            value = 0.0
            for n in chain[d].get(k, []):
                value = value + y_got[c, n, piece].astype(f32)
            return value

        def y_wait(k, d):
            for copy in copies.pop((k, d), []):
                copy.wait_recv()

        copies = {}
        for turn, edges in enumerate(sums(half_y)):
            if not y_first:
                i, block = over[turn]
                wait_shared(pair_got.at[c, pl.ds(0, len(block))], i)
            for k, k_to in edges:
                for d in (1, -1):
                    if k > length(half_y, c, d):
                        continue
                    n = k - 1 + (0 if d == 1 else half_y)
                    y_wait(k, d)
                    value = local_term(d * k) + y_sum(k, d, pieces)
                    y_send[c, n, pieces] = value.astype(bf16)
                    copy = send(
                        y_send.at[c, n, pieces], y_got.at[c, n, pieces], to_y[d * (k - k_to)], sems
                    )
                    chain[d].setdefault(k_to, []).append(n)
                    copies.setdefault((k_to, d), []).append(copy)
            yield
        for d in (1, -1):
            y_wait(0, d)
        if y_first:
            def total(piece):
                return terms[c, piece, y].astype(f32) + y_sum(0, 1, piece) + y_sum(0, -1, piece)

            last_send[c] = total(other_pair).astype(bf16)
            over = send(last_send.at[c], last_got.at[c], to_pair, 5)
            yield
            over.wait_recv()
            value = total(pair) + last_got[c].astype(f32)
        else:
            i, block = over[-1]
            wait_shared(pair_got.at[c, pl.ds(0, len(block))], i)
            value = local_term(0) + y_sum(0, 1, 0) + y_sum(0, -1, 0)
        grad_out[:, cols] = value.astype(bf16)

    near = list(range(half_z - 2, 0, -1))
    weight_term(half_z)
    for d in (1, -1):
        if half_z > 1:
            weight_term(d * (half_z - 1))
    ring = weight_ring()
    next(ring)
    running = []
    for c in range(chunks):
        g = scatter(c)
        next(g)
        running.append(g)
        if near and c == chunks // 2:
            for d in (1, -1):
                weight_term(d * near[0])
    for g in running[SCATTER_YX:]:
        next(g)
    for k in near[1:]:
        for d in (1, -1):
            weight_term(d * k)
    weight_term(0)
    running.insert(0, ring)
    while running:
        for g in list(running):
            if next(g, running) is running:
                running.remove(g)

    far = ring_y - 1
    wait_group(0, tokens.at[pl.ds(0, GATHER_XY), 0, 0])
    wait_group(1, tokens.at[pl.ds(0, GATHER_XY), :, pl.ds(0, far)])
    wait_group(2, tokens.at[pl.ds(GATHER_XY, chunks - GATHER_XY), 0, pl.ds(0, far)])
    wait_group(3, tokens.at[pl.ds(GATHER_XY, chunks - GATHER_XY), 0])
    wait_group(4, terms.at[pl.ds(0, SCATTER_YX), :, pl.ds(0, far)])
    wait_group(5, terms.at[pl.ds(0, SCATTER_YX), 0, 0])
    wait_group(6, terms.at[pl.ds(SCATTER_YX, chunks - SCATTER_YX), 0, pl.ds(0, far)])
    wait_group(7, terms.at[pl.ds(SCATTER_YX, chunks - SCATTER_YX), 0])
    wait_group(8, core_got)
    wait_group(9, core_got.at[pl.ds(0, ring_z - 1)])
    wait_group(10, x_send)


def store(*refs):
    copies = [pltpu.make_async_copy(refs[i], refs[i + 3], refs[6].at[i]) for i in range(3)]
    for copy in copies:
        copy.start()
    for copy in copies:
        copy.wait()


def local(normed, w_query, query_gain, query_cot):
    ring_y = lax.axis_size("mp") // PAIR
    ring_z = lax.axis_size("dp") // (CORES * ACROSS)
    rows, features = normed.shape
    tok, columns = query_cot.shape
    chunks, width, group = CHUNKS, features // CHUNKS, features // ring_z
    own_rows = group // (ACROSS * CORES)
    bf16, f32 = jnp.bfloat16, jnp.float32
    vmem, hbm = pl.BlockSpec(memory_space=pltpu.VMEM), pl.BlockSpec(memory_space=pltpu.HBM)
    y_count, z_count = ring_y - 1, ring_z - 1
    children, _ = spread(ring_y // 2)
    first = sum(t <= m for m in (ring_y // 2, ring_y // 2 - 1) for t in children[0])
    copies = GATHER_XY * (1 + y_count + first) + (chunks - GATHER_XY) * (y_count + 1)
    copies += SCATTER_YX * (y_count + 1) + ring_z + ACROSS * z_count + ACROSS - 1
    copies += (chunks - SCATTER_YX) * (y_count + len(blocks_by_turn(ring_y // 2)))
    outs = pl.pallas_call(
        functools.partial(kernel, (ring_y, ring_z, rows, features, columns)),
        out_shape=(
            jax.ShapeDtypeStruct((tok, columns), bf16),
            jax.ShapeDtypeStruct((rows, features), bf16),
            jax.ShapeDtypeStruct((own_rows, columns), f32),
        ),
        in_specs=[hbm, hbm, vmem, hbm],
        out_specs=(vmem, vmem, vmem),
        scratch_shapes=[
            pltpu.VMEM((chunks, PAIR, ring_y, rows, width), bf16),
            pltpu.VMEM((ring_z, group, tok), bf16),
            pltpu.VMEM((features, columns), bf16),
            pltpu.VMEM((tok, columns), bf16),
            pltpu.VMEM((tok, columns), f32),
            pltpu.VMEM((tok, columns), bf16),
            pltpu.VMEM((chunks, PAIR, ring_y, rows, width), bf16),
            pltpu.VMEM((ring_z, ACROSS, CORES, own_rows, columns), f32),
            pltpu.VMEM((ring_z, ACROSS, CORES, own_rows, columns), bf16),
            pltpu.VMEM((ring_z, ACROSS, own_rows, columns), bf16),
            pltpu.VMEM((ring_z, ACROSS, own_rows, columns), bf16),
            pltpu.VMEM((ring_z, ACROSS, own_rows, columns), bf16),
            pltpu.VMEM((ACROSS - 1, own_rows, columns), bf16),
            pltpu.VMEM((ACROSS - 1, own_rows, columns), bf16),
            pltpu.VMEM((chunks, ring_y, PAIR, rows, width), bf16),
            pltpu.VMEM((chunks, ring_y, PAIR, rows, width), bf16),
            pltpu.VMEM((chunks, ring_y, rows, width), bf16),
            pltpu.VMEM((chunks, rows, width), bf16),
            pltpu.VMEM((chunks, rows, width), bf16),
            pltpu.SemaphoreType.DMA((3,)),
            pltpu.SemaphoreType.DMA((11,)),
            pltpu.SemaphoreType.DMA((copies,)),
        ],
        compiler_params=pltpu.CompilerParams(
            collective_id=0, has_side_effects=True, vmem_limit_bytes=44 * 2**20
        ),
    )(*(pltpu.with_memory_space_constraint(a, pltpu.HBM) for a in (normed, w_query, query_gain, query_cot)))

    return pl.pallas_call(
        store,
        out_shape=[jax.ShapeDtypeStruct(o.shape, o.dtype) for o in outs],
        in_specs=[vmem] * 3,
        out_specs=[pl.BlockSpec(memory_space=pl.ANY)] * 3,
        scratch_shapes=[pltpu.SemaphoreType.DMA((3,))],
    )(*(pltpu.with_memory_space_constraint(o, pltpu.VMEM) for o in outs))


def solution(mesh):
    return jax.shard_map(
        local,
        mesh=mesh,
        in_specs=(P(("dp", "mp"), None), P(None, "mp"), P("mp"), P("dp", "mp")),
        out_specs=(P("dp", "mp"), P(("dp", "mp"), None), P("dp", "mp")),
        check_vma=False,
    )
```

```python
import functools
import itertools

import jax
import jax.numpy as jnp
from jax import lax
from jax.experimental import pallas as pl
from jax.experimental.pallas import tpu as pltpu
from jax.sharding import PartitionSpec as P

HEAD = 128
PAIR = 2
CORES = 2
ACROSS = 4
MESH = pl.DeviceIdType.MESH
CHUNKS = 4
GATHER_XY = 1
SCATTER_YX = 2


NEAR = [[(4, 3)], [(3, 2)], [(2, 1)], [(1, 0)]]
MIXED = [[(4, 2), (3, 2)], [(2, 1)], [(1, 0)]]
FAR = [[(4, 2), (3, 2), (1, 0)], [(2, 0)]]
GATHER_ROUTES = (FAR, NEAR)
SCATTER_ROUTES = (MIXED, NEAR)
WEIGHT_ROUTES = (MIXED, NEAR)


def sums(half, route):
    if half == 4:
        return route
    return [[(k, k - 1)] for k in range(half, 0, -1)]


def blocks_by_turn(half, route):
    rounds = [
        [k * d for k, _ in edges for d in ((1,) if k == half else (1, -1))] for edges in sums(half, route)
    ]
    return rounds + [[0]]


def spread(half, route):
    edges = [(b, a) for now in sums(half, route) for a, b in now]
    children = {k: sorted((b for a, b in edges if a == k), reverse=True) for k in range(half + 1)}
    arrivals, now = [], children[0]
    while now:
        arrivals.append(now)
        now = [b for a in now for b in children[a]]
    return children, arrivals


def kernel(
    dims, normed, w_hbm, gain, cot_hbm, queries_out, grad_out, weight_out,
    tokens, turned, w, cot, proj, pre, terms, term_mine, term_sent, core_got,
    z_send, z_got, x_send, x_got, y_send, y_got, pair_got, last_send, last_got,
    local_sem, send_sem, recv_sem,
):
    ring_y, ring_z, rows, features, columns = dims
    half_y, half_z = ring_y // 2, ring_z // 2
    chunks, width, group = CHUNKS, features // CHUNKS, features // ring_z
    own_rows = group // (ACROSS * CORES)
    tok = PAIR * ring_y * rows
    f32, bf16 = jnp.float32, jnp.bfloat16
    dp, mp = lax.axis_index("dp"), lax.axis_index("mp")
    pair, y = mp // ring_y, lax.rem(mp, ring_y)
    core = lax.rem(dp, CORES)
    across = lax.rem(dp // CORES, ACROSS)
    z = dp // (CORES * ACROSS)
    other_pair, other_core = 1 - pair, 1 - core

    def at_y(step):
        return lax.rem(y + step + ring_y, ring_y)

    def at_z(step):
        return lax.rem(z + step + ring_z, ring_z)

    def at_across(step):
        return lax.rem(across + step, ACROSS)

    def dp_of(zz, xx, cc):
        return (zz * ACROSS + xx) * CORES + cc

    to_pair = (dp, other_pair * ring_y + y)
    to_core = (dp_of(z, across, other_core), mp)
    steps_y, steps_z = [[-2, -1, 1, 2] if half > 2 else [-1, 1] for half in (half_y, half_z)]
    to_y = {k: (dp, pair * ring_y + at_y(k)) for k in steps_y}
    to_z = {k: (dp_of(at_z(k), across, core), mp) for k in steps_z}
    to_across = {j: (dp_of(z, at_across(j), core), mp) for j in range(1, ACROSS)}

    counts = [None]

    def remote(src, dst, device, group, i):
        return pltpu.make_async_remote_copy(
            src_ref=src, dst_ref=dst, send_sem=send_sem.at[group], recv_sem=recv_sem.at[i],
            device_id=device, device_id_type=MESH,
        )

    def send(src, dst, device, group, i=None):
        copy = remote(src, dst, device, group, next(counts[0]) if i is None else i)
        copy.start()
        return copy

    def wait_shared(view, i):
        remote(view, view, to_core, 0, i).wait_recv()

    def wait_group(group, view):
        remote(view, view, to_core, group, 0).wait_send()

    def length(half, index, d):
        return half if (d == 1) == (index % 2 == 0) else half - 1

    w_in = pltpu.make_async_copy(w_hbm, w, local_sem.at[1])
    cot_in = pltpu.make_async_copy(cot_hbm, cot, local_sem.at[2])
    for c in range(chunks):
        pltpu.make_async_copy(
            normed.at[:, pl.ds(c * width, width)], tokens.at[c, pair, y], local_sem.at[0]
        ).start()
    w_in.start()
    cot_in.start()

    barrier = pltpu.get_barrier_semaphore()
    peers = [to_pair, to_core, *to_y.values(), *to_z.values(), *to_across.values()]
    for peer in peers:
        pl.semaphore_signal(barrier, inc=1, device_id=peer, device_id_type=MESH)
    own = tokens.at[:, pair, y]
    pltpu.make_async_copy(own, own, local_sem.at[0]).wait()
    pl.semaphore_wait(barrier, len(peers))

    def work(gather_route, scatter_route, weight_route):
        counts[0] = itertools.count(ring_z)

        children, arrivals = spread(half_y, gather_route)

        def onward(views, k, d, c, group):
            return {
                t: [send(view, view, to_y[d * (t - k)], group) for view in views]
                for t in children[k]
                if t <= length(half_y, c, d)
            }

        def gather_xy(c):
            mine, theirs = tokens.at[c, pair, y], tokens.at[c, other_pair, y]
            over = send(mine, mine, to_pair, 0)
            chain = {d: onward([mine], 0, d, c, 1) for d in (1, -1)}
            yield
            over.wait_recv()
            for d in chain:
                for t, copies in onward([theirs], 0, d, c, 1).items():
                    chain[d][t] += copies
            yield
            for now in arrivals:
                for t in now:
                    for d in chain:
                        if t in chain[d]:
                            for copy in chain[d][t]:
                                copy.wait_recv()
                            chain[d].update(onward([tokens.at[c, :, at_y(-d * t)]], t, d, c, 1))
                yield

        def gather_yx(c):
            mine = tokens.at[c, pair, y]
            chain = {d: onward([mine], 0, d, c, 2) for d in (1, -1)}
            over = next(counts[0])
            send(mine, mine, to_pair, 3, over)
            yield
            for now in arrivals:
                for t in now:
                    for d in chain:
                        if t in chain[d]:
                            chain[d][t][0].wait_recv()
                            view = tokens.at[c, pair, at_y(-d * t)]
                            chain[d].update(onward([view], t, d, c, 2))
                            send(view, view, to_pair, 3, over)
                yield
            wait_shared(tokens.at[c, other_pair], over)

        def project(c):
            got = tokens[c].reshape(tok, width)
            term = jnp.dot(got, w[pl.ds(c * width, width), :], preferred_element_type=f32)
            if c == 0:
                proj[...] = term
            else:
                proj[...] += term
            per = width // group
            turned[pl.ds(c * per, per)] = got.T.reshape(per, group, tok)

        gathers = [(gather_xy if c < GATHER_XY else gather_yx)(c) for c in range(chunks)]
        for _ in range(len(arrivals) + 2):
            for g in gathers[GATHER_XY:] + gathers[:GATHER_XY]:
                next(g, None)
        w_in.wait()
        for c in range(chunks):
            for _ in gathers[c]:
                pass
            project(c)

        cot_in.wait()
        for head in range(columns // HEAD):
            cols = pl.ds(head * HEAD, HEAD)
            values = proj[:, cols]
            centred = values - jnp.mean(values, axis=-1, keepdims=True)
            spread_inv = lax.rsqrt(jnp.mean(centred * centred, axis=-1, keepdims=True) + 1e-06)
            unit = centred * spread_inv
            queries_out[:, cols] = (unit * gain[cols]).astype(bf16)
            scaled = cot[:, cols].astype(f32) * gain[cols]
            grad = spread_inv * (
                scaled
                - jnp.mean(scaled, axis=-1, keepdims=True)
                - unit * jnp.mean(scaled * unit, axis=-1, keepdims=True)
            )
            pre[:, cols] = grad.astype(bf16)

        core_copy = {}

        def slot(step):
            return step % ring_z

        def weight_term(step):
            i = slot(step)
            term = jnp.dot(turned[at_z(step)], pre[...], preferred_element_type=f32)
            term = term.reshape(ACROSS, CORES, own_rows, columns)
            term_mine[i] = term
            term_sent[i] = term.astype(bf16)
            core_copy[i] = send(term_sent.at[i, :, other_core], core_got.at[i], to_core, 8, i)

        arrived = set()

        def chip_term(step, block):
            i = slot(step)
            if i not in arrived:
                arrived.add(i)
                core_copy[i].wait_recv()
            return term_mine[i, block, core] + core_got[i, block].astype(f32)

        order_across = [2, 1, 3, 0][:ACROSS] if ACROSS == 4 else list(range(ACROSS - 1, -1, -1))

        def z_sum(chain, k, d, block):
            value = 0.0
            for n, copy in chain.get(k, []):
                copy.wait_recv()
                value = value + z_got[n, block].astype(f32)
            return value

        def weight_ring():
            chain = {(j, d): {} for j in order_across for d in (1, -1)}
            rounds = sums(half_z, weight_route)
            over = {}

            def one_round(index, turn):
                j = order_across[index]
                block = at_across(j)
                for k, k_to in (rounds + [[]])[turn]:
                    for d in (1, -1):
                        if k > length(half_z, index, d):
                            continue
                        n = k - 1 + (0 if d == 1 else half_z)
                        value = chip_term(d * k, block) + z_sum(chain[j, d], k, d, block)
                        z_send[n, block] = value.astype(bf16)
                        copy = send(z_send.at[n, block], z_got.at[n, block], to_z[d * (k - k_to)], 9)
                        chain[j, d].setdefault(k_to, []).append((n, copy))
                if turn == len(rounds):
                    value = chip_term(0, block)
                    for d in (1, -1):
                        value = value + z_sum(chain[j, d], 0, d, block)
                    if j:
                        x_send[j - 1] = value.astype(bf16)
                        over[j] = send(x_send.at[j - 1], x_got.at[j - 1], to_across[j], 10)
                    else:
                        over[0] = value

            for turn in range(len(rounds) + 1):
                for index in range(ACROSS):
                    one_round(index, turn)
                yield
            total = over.pop(0)
            for j, copy in over.items():
                copy.wait_recv()
                total = total + x_got[j - 1].astype(f32)
            weight_out[...] = total

        def scatter(c):
            y_first = c < SCATTER_YX
            cols = pl.ds(c * width, width)
            term = lax.dot_general(
                pre[...], w[cols, :], (((1,), (1,)), ((), ())), preferred_element_type=f32
            )
            terms[c] = term.astype(bf16).reshape(PAIR, ring_y, rows, width)
            pieces = pl.ds(0, PAIR) if y_first else 0
            sems = 4 if y_first else 6

            def local_term(step):
                if y_first:
                    return terms[c, :, at_y(step)].astype(f32)
                return terms[c, pair, at_y(step)].astype(f32) + pair_got[c, at_y(step)].astype(f32)

            if not y_first:
                over = [(next(counts[0]), block) for block in blocks_by_turn(half_y, scatter_route)]
                for turn, (i, block) in enumerate(over):
                    if turn == 1:
                        yield
                    for r in block:
                        send(terms.at[c, other_pair, at_y(r)], pair_got.at[c, at_y(r)], to_pair, 7, i)
                yield
            chain = {d: {} for d in (1, -1)}

            def y_sum(k, d, piece):
                value = 0.0
                for n in chain[d].get(k, []):
                    value = value + y_got[c, n, piece].astype(f32)
                return value

            def y_wait(k, d):
                for copy in copies.pop((k, d), []):
                    copy.wait_recv()

            copies = {}
            for turn, edges in enumerate(sums(half_y, scatter_route)):
                if not y_first:
                    i, block = over[turn]
                    wait_shared(pair_got.at[c, pl.ds(0, len(block))], i)
                for k, k_to in edges:
                    for d in (1, -1):
                        if k > length(half_y, c, d):
                            continue
                        n = k - 1 + (0 if d == 1 else half_y)
                        y_wait(k, d)
                        value = local_term(d * k) + y_sum(k, d, pieces)
                        y_send[c, n, pieces] = value.astype(bf16)
                        copy = send(
                            y_send.at[c, n, pieces], y_got.at[c, n, pieces], to_y[d * (k - k_to)], sems
                        )
                        chain[d].setdefault(k_to, []).append(n)
                        copies.setdefault((k_to, d), []).append(copy)
                yield
            for d in (1, -1):
                y_wait(0, d)
            if y_first:
                def total(piece):
                    return terms[c, piece, y].astype(f32) + y_sum(0, 1, piece) + y_sum(0, -1, piece)

                last_send[c] = total(other_pair).astype(bf16)
                over = send(last_send.at[c], last_got.at[c], to_pair, 5)
                yield
                over.wait_recv()
                value = total(pair) + last_got[c].astype(f32)
            else:
                i, block = over[-1]
                wait_shared(pair_got.at[c, pl.ds(0, len(block))], i)
                value = local_term(0) + y_sum(0, 1, 0) + y_sum(0, -1, 0)
            grad_out[:, cols] = value.astype(bf16)

        near = list(range(half_z - 2, 0, -1))
        weight_term(half_z)
        for d in (1, -1):
            if half_z > 1:
                weight_term(d * (half_z - 1))
        ring = weight_ring()
        next(ring)
        running = []
        for c in range(chunks):
            g = scatter(c)
            next(g)
            running.append(g)
            if near and c == chunks // 2:
                for d in (1, -1):
                    weight_term(d * near[0])
        for g in running[SCATTER_YX:]:
            next(g)
        for k in near[1:]:
            for d in (1, -1):
                weight_term(d * k)
        weight_term(0)
        running.insert(0, ring)
        while running:
            for g in list(running):
                if next(g, running) is running:
                    running.remove(g)

    for which in range(CORES):

        @pl.when(core == which)
        def _(which=which):
            work(GATHER_ROUTES[which], SCATTER_ROUTES[which], WEIGHT_ROUTES[which])

    far = ring_y - 1
    wait_group(0, tokens.at[pl.ds(0, GATHER_XY), 0, 0])
    wait_group(1, tokens.at[pl.ds(0, GATHER_XY), :, pl.ds(0, far)])
    wait_group(2, tokens.at[pl.ds(GATHER_XY, chunks - GATHER_XY), 0, pl.ds(0, far)])
    wait_group(3, tokens.at[pl.ds(GATHER_XY, chunks - GATHER_XY), 0])
    wait_group(4, terms.at[pl.ds(0, SCATTER_YX), :, pl.ds(0, far)])
    wait_group(5, terms.at[pl.ds(0, SCATTER_YX), 0, 0])
    wait_group(6, terms.at[pl.ds(SCATTER_YX, chunks - SCATTER_YX), 0, pl.ds(0, far)])
    wait_group(7, terms.at[pl.ds(SCATTER_YX, chunks - SCATTER_YX), 0])
    wait_group(8, core_got)
    wait_group(9, core_got.at[pl.ds(0, ring_z - 1)])
    wait_group(10, x_send)


def store(*refs):
    copies = [pltpu.make_async_copy(refs[i], refs[i + 3], refs[6].at[i]) for i in range(3)]
    for copy in copies:
        copy.start()
    for copy in copies:
        copy.wait()


def local(normed, w_query, query_gain, query_cot):
    ring_y = lax.axis_size("mp") // PAIR
    ring_z = lax.axis_size("dp") // (CORES * ACROSS)
    rows, features = normed.shape
    tok, columns = query_cot.shape
    chunks, width, group = CHUNKS, features // CHUNKS, features // ring_z
    own_rows = group // (ACROSS * CORES)
    bf16, f32 = jnp.bfloat16, jnp.float32
    vmem, hbm = pl.BlockSpec(memory_space=pltpu.VMEM), pl.BlockSpec(memory_space=pltpu.HBM)
    y_count, z_count = ring_y - 1, ring_z - 1
    most = 2 * len(FAR[0])
    copies = GATHER_XY * (1 + y_count + most) + (chunks - GATHER_XY) * (y_count + 1)
    copies += SCATTER_YX * (y_count + 1) + (chunks - SCATTER_YX) * (y_count + ring_y // 2 + 1)
    copies += ring_z + ACROSS * z_count + ACROSS - 1
    outs = pl.pallas_call(
        functools.partial(kernel, (ring_y, ring_z, rows, features, columns)),
        out_shape=(
            jax.ShapeDtypeStruct((tok, columns), bf16),
            jax.ShapeDtypeStruct((rows, features), bf16),
            jax.ShapeDtypeStruct((own_rows, columns), f32),
        ),
        in_specs=[hbm, hbm, vmem, hbm],
        out_specs=(vmem, vmem, vmem),
        scratch_shapes=[
            pltpu.VMEM((chunks, PAIR, ring_y, rows, width), bf16),
            pltpu.VMEM((ring_z, group, tok), bf16),
            pltpu.VMEM((features, columns), bf16),
            pltpu.VMEM((tok, columns), bf16),
            pltpu.VMEM((tok, columns), f32),
            pltpu.VMEM((tok, columns), bf16),
            pltpu.VMEM((chunks, PAIR, ring_y, rows, width), bf16),
            pltpu.VMEM((ring_z, ACROSS, CORES, own_rows, columns), f32),
            pltpu.VMEM((ring_z, ACROSS, CORES, own_rows, columns), bf16),
            pltpu.VMEM((ring_z, ACROSS, own_rows, columns), bf16),
            pltpu.VMEM((ring_z, ACROSS, own_rows, columns), bf16),
            pltpu.VMEM((ring_z, ACROSS, own_rows, columns), bf16),
            pltpu.VMEM((ACROSS - 1, own_rows, columns), bf16),
            pltpu.VMEM((ACROSS - 1, own_rows, columns), bf16),
            pltpu.VMEM((chunks, ring_y, PAIR, rows, width), bf16),
            pltpu.VMEM((chunks, ring_y, PAIR, rows, width), bf16),
            pltpu.VMEM((chunks, ring_y, rows, width), bf16),
            pltpu.VMEM((chunks, rows, width), bf16),
            pltpu.VMEM((chunks, rows, width), bf16),
            pltpu.SemaphoreType.DMA((3,)),
            pltpu.SemaphoreType.DMA((11,)),
            pltpu.SemaphoreType.DMA((copies,)),
        ],
        compiler_params=pltpu.CompilerParams(
            collective_id=0, has_side_effects=True, vmem_limit_bytes=44 * 2**20
        ),
    )(*(pltpu.with_memory_space_constraint(a, pltpu.HBM) for a in (normed, w_query, query_gain, query_cot)))

    return pl.pallas_call(
        store,
        out_shape=[jax.ShapeDtypeStruct(o.shape, o.dtype) for o in outs],
        in_specs=[vmem] * 3,
        out_specs=[pl.BlockSpec(memory_space=pl.ANY)] * 3,
        scratch_shapes=[pltpu.SemaphoreType.DMA((3,))],
    )(*(pltpu.with_memory_space_constraint(o, pltpu.VMEM) for o in outs))


def solution(mesh):
    return jax.shard_map(
        local,
        mesh=mesh,
        in_specs=(P(("dp", "mp"), None), P(None, "mp"), P("mp"), P("dp", "mp")),
        out_specs=(P("dp", "mp"), P(("dp", "mp"), None), P("dp", "mp")),
        check_vma=False,
    )
```

```python
import functools
import itertools

import jax
import jax.numpy as jnp
from jax import lax
from jax.experimental import pallas as pl
from jax.experimental.pallas import tpu as pltpu
from jax.sharding import PartitionSpec as P

HEAD = 128
PAIR = 2
CORES = 2
ACROSS = 4
MESH = pl.DeviceIdType.MESH
CHUNKS = 4
GATHER_XY = 1
SCATTER_YX = 2


NEAR = [[(4, 3)], [(3, 2)], [(2, 1)], [(1, 0)]]
MIXED = [[(4, 2), (3, 2)], [(2, 1)], [(1, 0)]]
FAR = [[(4, 2), (3, 2), (1, 0)], [(2, 0)]]
GATHER_ROUTES = (FAR, NEAR)
SCATTER_ROUTES = (MIXED, MIXED)
WEIGHT_ROUTES = (MIXED, NEAR)


def sums(half, route):
    if half == 4:
        return route
    return [[(k, k - 1)] for k in range(half, 0, -1)]


def blocks_by_turn(half, route):
    rounds = [
        [k * d for k, _ in edges for d in ((1,) if k == half else (1, -1))] for edges in sums(half, route)
    ]
    return rounds + [[0]]


def spread(half, route):
    edges = [(b, a) for now in sums(half, route) for a, b in now]
    children = {k: sorted((b for a, b in edges if a == k), reverse=True) for k in range(half + 1)}
    arrivals, now = [], children[0]
    while now:
        arrivals.append(now)
        now = [b for a in now for b in children[a]]
    return children, arrivals


def kernel(
    dims, normed, w_hbm, gain, cot_hbm, queries_out, grad_out, weight_out,
    tokens, turned, w, cot, proj, pre, terms, term_mine, term_sent, core_got,
    z_send, z_got, x_send, x_got, y_send, y_got, pair_got, last_send, last_got,
    local_sem, send_sem, recv_sem,
):
    ring_y, ring_z, rows, features, columns = dims
    half_y, half_z = ring_y // 2, ring_z // 2
    chunks, width, group = CHUNKS, features // CHUNKS, features // ring_z
    own_rows = group // (ACROSS * CORES)
    tok = PAIR * ring_y * rows
    f32, bf16 = jnp.float32, jnp.bfloat16
    dp, mp = lax.axis_index("dp"), lax.axis_index("mp")
    pair, y = mp // ring_y, lax.rem(mp, ring_y)
    core = lax.rem(dp, CORES)
    across = lax.rem(dp // CORES, ACROSS)
    z = dp // (CORES * ACROSS)
    other_pair, other_core = 1 - pair, 1 - core

    def at_y(step):
        return lax.rem(y + step + ring_y, ring_y)

    def at_z(step):
        return lax.rem(z + step + ring_z, ring_z)

    def at_across(step):
        return lax.rem(across + step, ACROSS)

    def dp_of(zz, xx, cc):
        return (zz * ACROSS + xx) * CORES + cc

    to_pair = (dp, other_pair * ring_y + y)
    to_core = (dp_of(z, across, other_core), mp)
    steps_y, steps_z = [[-2, -1, 1, 2] if half > 2 else [-1, 1] for half in (half_y, half_z)]
    to_y = {k: (dp, pair * ring_y + at_y(k)) for k in steps_y}
    to_z = {k: (dp_of(at_z(k), across, core), mp) for k in steps_z}
    to_across = {j: (dp_of(z, at_across(j), core), mp) for j in range(1, ACROSS)}

    counts = [None]

    def remote(src, dst, device, group, i):
        return pltpu.make_async_remote_copy(
            src_ref=src, dst_ref=dst, send_sem=send_sem.at[group], recv_sem=recv_sem.at[i],
            device_id=device, device_id_type=MESH,
        )

    def send(src, dst, device, group, i=None):
        copy = remote(src, dst, device, group, next(counts[0]) if i is None else i)
        copy.start()
        return copy

    def wait_shared(view, i):
        remote(view, view, to_core, 0, i).wait_recv()

    def wait_group(group, view):
        remote(view, view, to_core, group, 0).wait_send()

    def length(half, index, d):
        return half if (d == 1) == (index % 2 == 0) else half - 1

    w_in = pltpu.make_async_copy(w_hbm, w, local_sem.at[1])
    cot_in = pltpu.make_async_copy(cot_hbm, cot, local_sem.at[2])
    for c in range(chunks):
        pltpu.make_async_copy(
            normed.at[:, pl.ds(c * width, width)], tokens.at[c, pair, y], local_sem.at[0]
        ).start()
    w_in.start()
    cot_in.start()

    barrier = pltpu.get_barrier_semaphore()
    peers = [to_pair, to_core, *to_y.values(), *to_z.values(), *to_across.values()]
    for peer in peers:
        pl.semaphore_signal(barrier, inc=1, device_id=peer, device_id_type=MESH)
    own = tokens.at[:, pair, y]
    pltpu.make_async_copy(own, own, local_sem.at[0]).wait()
    pl.semaphore_wait(barrier, len(peers))

    def work(gather_route, scatter_route, weight_route):
        counts[0] = itertools.count(ring_z)

        children, arrivals = spread(half_y, gather_route)

        def onward(views, k, d, c, group):
            return {
                t: [send(view, view, to_y[d * (t - k)], group) for view in views]
                for t in children[k]
                if t <= length(half_y, c, d)
            }

        def gather_xy(c):
            mine, theirs = tokens.at[c, pair, y], tokens.at[c, other_pair, y]
            over = send(mine, mine, to_pair, 0)
            chain = {d: onward([mine], 0, d, c, 1) for d in (1, -1)}
            yield
            over.wait_recv()
            for d in chain:
                for t, copies in onward([theirs], 0, d, c, 1).items():
                    chain[d][t] += copies
            yield
            for now in arrivals:
                for t in now:
                    for d in chain:
                        if t in chain[d]:
                            for copy in chain[d][t]:
                                copy.wait_recv()
                            chain[d].update(onward([tokens.at[c, :, at_y(-d * t)]], t, d, c, 1))
                yield

        def gather_yx(c):
            mine = tokens.at[c, pair, y]
            chain = {d: onward([mine], 0, d, c, 2) for d in (1, -1)}
            over = next(counts[0])
            send(mine, mine, to_pair, 3, over)
            yield
            for now in arrivals:
                for t in now:
                    for d in chain:
                        if t in chain[d]:
                            chain[d][t][0].wait_recv()
                            view = tokens.at[c, pair, at_y(-d * t)]
                            chain[d].update(onward([view], t, d, c, 2))
                            send(view, view, to_pair, 3, over)
                yield
            wait_shared(tokens.at[c, other_pair], over)

        def project(c):
            got = tokens[c].reshape(tok, width)
            term = jnp.dot(got, w[pl.ds(c * width, width), :], preferred_element_type=f32)
            if c == 0:
                proj[...] = term
            else:
                proj[...] += term
            per = width // group
            turned[pl.ds(c * per, per)] = got.T.reshape(per, group, tok)

        gathers = [(gather_xy if c < GATHER_XY else gather_yx)(c) for c in range(chunks)]
        for _ in range(len(arrivals) + 2):
            for g in gathers[GATHER_XY:] + gathers[:GATHER_XY]:
                next(g, None)
        w_in.wait()
        for c in range(chunks):
            for _ in gathers[c]:
                pass
            project(c)

        cot_in.wait()
        for head in range(columns // HEAD):
            cols = pl.ds(head * HEAD, HEAD)
            values = proj[:, cols]
            centred = values - jnp.mean(values, axis=-1, keepdims=True)
            spread_inv = lax.rsqrt(jnp.mean(centred * centred, axis=-1, keepdims=True) + 1e-06)
            unit = centred * spread_inv
            queries_out[:, cols] = (unit * gain[cols]).astype(bf16)
            scaled = cot[:, cols].astype(f32) * gain[cols]
            grad = spread_inv * (
                scaled
                - jnp.mean(scaled, axis=-1, keepdims=True)
                - unit * jnp.mean(scaled * unit, axis=-1, keepdims=True)
            )
            pre[:, cols] = grad.astype(bf16)

        core_copy = {}

        def slot(step):
            return step % ring_z

        def weight_term(step):
            i = slot(step)
            term = jnp.dot(turned[at_z(step)], pre[...], preferred_element_type=f32)
            term = term.reshape(ACROSS, CORES, own_rows, columns)
            term_mine[i] = term
            term_sent[i] = term.astype(bf16)
            core_copy[i] = send(term_sent.at[i, :, other_core], core_got.at[i], to_core, 8, i)

        arrived = set()

        def chip_term(step, block):
            i = slot(step)
            if i not in arrived:
                arrived.add(i)
                core_copy[i].wait_recv()
            return term_mine[i, block, core] + core_got[i, block].astype(f32)

        order_across = [2, 1, 3, 0][:ACROSS] if ACROSS == 4 else list(range(ACROSS - 1, -1, -1))

        def z_sum(chain, k, d, block):
            value = 0.0
            for n, copy in chain.get(k, []):
                copy.wait_recv()
                value = value + z_got[n, block].astype(f32)
            return value

        def weight_ring():
            chain = {(j, d): {} for j in order_across for d in (1, -1)}
            rounds = sums(half_z, weight_route)
            over = {}

            def one_round(index, turn):
                j = order_across[index]
                block = at_across(j)
                for k, k_to in (rounds + [[]])[turn]:
                    for d in (1, -1):
                        if k > length(half_z, index, d):
                            continue
                        n = k - 1 + (0 if d == 1 else half_z)
                        value = chip_term(d * k, block) + z_sum(chain[j, d], k, d, block)
                        z_send[n, block] = value.astype(bf16)
                        copy = send(z_send.at[n, block], z_got.at[n, block], to_z[d * (k - k_to)], 9)
                        chain[j, d].setdefault(k_to, []).append((n, copy))
                if turn == len(rounds):
                    value = chip_term(0, block)
                    for d in (1, -1):
                        value = value + z_sum(chain[j, d], 0, d, block)
                    if j:
                        x_send[j - 1] = value.astype(bf16)
                        over[j] = send(x_send.at[j - 1], x_got.at[j - 1], to_across[j], 10)
                    else:
                        over[0] = value

            for turn in range(len(rounds) + 1):
                for index in range(ACROSS):
                    one_round(index, turn)
                yield
            total = over.pop(0)
            for j, copy in over.items():
                copy.wait_recv()
                total = total + x_got[j - 1].astype(f32)
            weight_out[...] = total

        def scatter(c):
            y_first = c < SCATTER_YX
            cols = pl.ds(c * width, width)
            term = lax.dot_general(
                pre[...], w[cols, :], (((1,), (1,)), ((), ())), preferred_element_type=f32
            )
            terms[c] = term.astype(bf16).reshape(PAIR, ring_y, rows, width)
            pieces = pl.ds(0, PAIR) if y_first else 0
            sems = 4 if y_first else 6

            def local_term(step):
                if y_first:
                    return terms[c, :, at_y(step)].astype(f32)
                return terms[c, pair, at_y(step)].astype(f32) + pair_got[c, at_y(step)].astype(f32)

            if not y_first:
                over = [(next(counts[0]), block) for block in blocks_by_turn(half_y, scatter_route)]
                for turn, (i, block) in enumerate(over):
                    if turn == 1:
                        yield
                    for r in block:
                        send(terms.at[c, other_pair, at_y(r)], pair_got.at[c, at_y(r)], to_pair, 7, i)
                yield
            chain = {d: {} for d in (1, -1)}

            def y_sum(k, d, piece):
                value = 0.0
                for n in chain[d].get(k, []):
                    value = value + y_got[c, n, piece].astype(f32)
                return value

            def y_wait(k, d):
                for copy in copies.pop((k, d), []):
                    copy.wait_recv()

            copies = {}
            for turn, edges in enumerate(sums(half_y, scatter_route)):
                if not y_first:
                    i, block = over[turn]
                    wait_shared(pair_got.at[c, pl.ds(0, len(block))], i)
                for k, k_to in edges:
                    for d in (1, -1):
                        if k > length(half_y, c, d):
                            continue
                        n = k - 1 + (0 if d == 1 else half_y)
                        y_wait(k, d)
                        value = local_term(d * k) + y_sum(k, d, pieces)
                        y_send[c, n, pieces] = value.astype(bf16)
                        copy = send(
                            y_send.at[c, n, pieces], y_got.at[c, n, pieces], to_y[d * (k - k_to)], sems
                        )
                        chain[d].setdefault(k_to, []).append(n)
                        copies.setdefault((k_to, d), []).append(copy)
                yield
            for d in (1, -1):
                y_wait(0, d)
            if y_first:
                def total(piece):
                    return terms[c, piece, y].astype(f32) + y_sum(0, 1, piece) + y_sum(0, -1, piece)

                last_send[c] = total(other_pair).astype(bf16)
                over = send(last_send.at[c], last_got.at[c], to_pair, 5)
                yield
                over.wait_recv()
                value = total(pair) + last_got[c].astype(f32)
            else:
                i, block = over[-1]
                wait_shared(pair_got.at[c, pl.ds(0, len(block))], i)
                value = local_term(0) + y_sum(0, 1, 0) + y_sum(0, -1, 0)
            grad_out[:, cols] = value.astype(bf16)

        near = list(range(half_z - 2, 0, -1))
        weight_term(half_z)
        for d in (1, -1):
            if half_z > 1:
                weight_term(d * (half_z - 1))
        ring = weight_ring()
        next(ring)
        running = []
        for c in range(chunks):
            g = scatter(c)
            next(g)
            running.append(g)
            if near and c == chunks // 2:
                for d in (1, -1):
                    weight_term(d * near[0])
        for g in running[SCATTER_YX:]:
            next(g)
        for k in near[1:]:
            for d in (1, -1):
                weight_term(d * k)
        weight_term(0)
        running.insert(0, ring)
        while running:
            for g in list(running):
                if next(g, running) is running:
                    running.remove(g)

    for which in range(CORES):

        @pl.when(core == which)
        def _(which=which):
            work(GATHER_ROUTES[which], SCATTER_ROUTES[which], WEIGHT_ROUTES[which])

    far = ring_y - 1
    wait_group(0, tokens.at[pl.ds(0, GATHER_XY), 0, 0])
    wait_group(1, tokens.at[pl.ds(0, GATHER_XY), :, pl.ds(0, far)])
    wait_group(2, tokens.at[pl.ds(GATHER_XY, chunks - GATHER_XY), 0, pl.ds(0, far)])
    wait_group(3, tokens.at[pl.ds(GATHER_XY, chunks - GATHER_XY), 0])
    wait_group(4, terms.at[pl.ds(0, SCATTER_YX), :, pl.ds(0, far)])
    wait_group(5, terms.at[pl.ds(0, SCATTER_YX), 0, 0])
    wait_group(6, terms.at[pl.ds(SCATTER_YX, chunks - SCATTER_YX), 0, pl.ds(0, far)])
    wait_group(7, terms.at[pl.ds(SCATTER_YX, chunks - SCATTER_YX), 0])
    wait_group(8, core_got)
    wait_group(9, core_got.at[pl.ds(0, ring_z - 1)])
    wait_group(10, x_send)


def store(*refs):
    copies = [pltpu.make_async_copy(refs[i], refs[i + 3], refs[6].at[i]) for i in range(3)]
    for copy in copies:
        copy.start()
    for copy in copies:
        copy.wait()


def local(normed, w_query, query_gain, query_cot):
    ring_y = lax.axis_size("mp") // PAIR
    ring_z = lax.axis_size("dp") // (CORES * ACROSS)
    rows, features = normed.shape
    tok, columns = query_cot.shape
    chunks, width, group = CHUNKS, features // CHUNKS, features // ring_z
    own_rows = group // (ACROSS * CORES)
    bf16, f32 = jnp.bfloat16, jnp.float32
    vmem, hbm = pl.BlockSpec(memory_space=pltpu.VMEM), pl.BlockSpec(memory_space=pltpu.HBM)
    y_count, z_count = ring_y - 1, ring_z - 1
    most = 2 * len(FAR[0])
    copies = GATHER_XY * (1 + y_count + most) + (chunks - GATHER_XY) * (y_count + 1)
    copies += SCATTER_YX * (y_count + 1) + (chunks - SCATTER_YX) * (y_count + ring_y // 2 + 1)
    copies += ring_z + ACROSS * z_count + ACROSS - 1
    outs = pl.pallas_call(
        functools.partial(kernel, (ring_y, ring_z, rows, features, columns)),
        out_shape=(
            jax.ShapeDtypeStruct((tok, columns), bf16),
            jax.ShapeDtypeStruct((rows, features), bf16),
            jax.ShapeDtypeStruct((own_rows, columns), f32),
        ),
        in_specs=[hbm, hbm, vmem, hbm],
        out_specs=(vmem, vmem, vmem),
        scratch_shapes=[
            pltpu.VMEM((chunks, PAIR, ring_y, rows, width), bf16),
            pltpu.VMEM((ring_z, group, tok), bf16),
            pltpu.VMEM((features, columns), bf16),
            pltpu.VMEM((tok, columns), bf16),
            pltpu.VMEM((tok, columns), f32),
            pltpu.VMEM((tok, columns), bf16),
            pltpu.VMEM((chunks, PAIR, ring_y, rows, width), bf16),
            pltpu.VMEM((ring_z, ACROSS, CORES, own_rows, columns), f32),
            pltpu.VMEM((ring_z, ACROSS, CORES, own_rows, columns), bf16),
            pltpu.VMEM((ring_z, ACROSS, own_rows, columns), bf16),
            pltpu.VMEM((ring_z, ACROSS, own_rows, columns), bf16),
            pltpu.VMEM((ring_z, ACROSS, own_rows, columns), bf16),
            pltpu.VMEM((ACROSS - 1, own_rows, columns), bf16),
            pltpu.VMEM((ACROSS - 1, own_rows, columns), bf16),
            pltpu.VMEM((chunks, ring_y, PAIR, rows, width), bf16),
            pltpu.VMEM((chunks, ring_y, PAIR, rows, width), bf16),
            pltpu.VMEM((chunks, ring_y, rows, width), bf16),
            pltpu.VMEM((chunks, rows, width), bf16),
            pltpu.VMEM((chunks, rows, width), bf16),
            pltpu.SemaphoreType.DMA((3,)),
            pltpu.SemaphoreType.DMA((11,)),
            pltpu.SemaphoreType.DMA((copies,)),
        ],
        compiler_params=pltpu.CompilerParams(
            collective_id=0, has_side_effects=True, vmem_limit_bytes=44 * 2**20
        ),
    )(*(pltpu.with_memory_space_constraint(a, pltpu.HBM) for a in (normed, w_query, query_gain, query_cot)))

    return pl.pallas_call(
        store,
        out_shape=[jax.ShapeDtypeStruct(o.shape, o.dtype) for o in outs],
        in_specs=[vmem] * 3,
        out_specs=[pl.BlockSpec(memory_space=pl.ANY)] * 3,
        scratch_shapes=[pltpu.SemaphoreType.DMA((3,))],
    )(*(pltpu.with_memory_space_constraint(o, pltpu.VMEM) for o in outs))


def solution(mesh):
    return jax.shard_map(
        local,
        mesh=mesh,
        in_specs=(P(("dp", "mp"), None), P(None, "mp"), P("mp"), P("dp", "mp")),
        out_specs=(P("dp", "mp"), P(("dp", "mp"), None), P("dp", "mp")),
        check_vma=False,
    )
```
